32 devices in a mesh: req: 8 (over z, x), head: 4 (over y, core).
Axes of the slice: x: 2, y: 2, z: 4, core: 2. Of those that a mesh axis runs over, the one named last changes fastest.
Arguments:
- query_new: bfloat16 [512, 5120], P('req', 'head'), may hold values from -6 to 6
- key_new: bfloat16 [512, 5120], P('req', 'head'), may hold values from -6 to 6
- value_new: bfloat16 [512, 5120], P('req', 'head'), may hold values from -6 to 6
- key_pool: bfloat16 [28288, 5120], P('req', 'head'), may hold values from -368 to 368
- value_pool: bfloat16 [28288, 5120], P('req', 'head'), may hold values from -6 to 6
- lengths: int32 [512], replicated, may hold values from 8 to 1024, as said below
- slot_request: int32 [512], replicated, may hold values from 0 to 511, as said below
- residual: bfloat16 [512, 5120], P(None, 'req'), may hold values from -6 to 6
- out_proj: bfloat16 [5120, 5120], P('head', 'req'), may hold values from -0.15625 to 0.15625
- norm_gain: bfloat16 [5120], replicated, may hold values from 0.5 to 1.5
- gate_proj: bfloat16 [5120, 13824], P(None, ('req', 'head')), may hold values from -0.078125 to 0.078125
- up_proj: bfloat16 [5120, 13824], P(None, ('req', 'head')), may hold values from -0.078125 to 0.078125
- down_proj: bfloat16 [13824, 5120], P('req', 'head'), may hold values from -0.21875 to 0.21875
Outputs:
- attended: bfloat16 [512, 5120], P('head', 'req')
- ffn_out: bfloat16 [512, 5120], P('req', 'head')
The draws below stay inside these ranges and needn't reach their ends.
Inputs may be any that keep to these rules, and one draw needn't show every extreme that they name: `slot_request`: a permutation of the requests; the 8 requests with more than 24 cached tokens sit two to an owner, on 4 owners. `lengths`: exactly 8 requests have 1024 // 2 to 1024 cached tokens and one of them has 1024; every other request has 8 to 24.
All inputs are finite; a program needn't handle non-finite values.
Results may differ from the reference program's by a relative error of at most 0.017.
Values may be sent and summed in bfloat16 or wider, within the bound.
A program may use at most 192 MiB of HBM per device.

```python
import math
import jax
import jax.numpy as jnp
from jax import lax

D = 5120
H = 40
HD = 128
FF = 13824
REQ_DEV = 64
LONG_MAX = 1024
SHORT_MAX = 24
NLONG = 8
REQS = 512
POOL = 3536
POOL_ALL = 28288
N_REQ = 8


def placement_tables(key):
    mixed_key = jax.random.fold_in(key, 11)
    key_order, key_hosts, key_offsets, key_short, key_long = jax.random.split(mixed_key, 5)
    slot_order = jax.random.permutation(key_order, REQS).astype(jnp.int32)
    long_hosts = jax.random.permutation(key_hosts, N_REQ)[:NLONG // 2].astype(jnp.int32)
    offsets = jax.random.permutation(key_offsets, REQ_DEV)[:2].astype(jnp.int32)
    long_slots = (long_hosts[:, None] * REQ_DEV + offsets[None, :]).reshape(-1)
    long_req = jnp.take(slot_order, long_slots)
    short_len = jax.random.randint(key_short, (REQS,), SHORT_MAX // 3, SHORT_MAX + 1, dtype=jnp.int32)
    long_len = jax.random.randint(key_long, (NLONG,), LONG_MAX // 2, LONG_MAX + 1, dtype=jnp.int32)
    long_len = long_len.at[0].set(LONG_MAX)
    return (slot_order, short_len.at[long_req].set(long_len))


def draw_lengths(key, part):
    return placement_tables(key)[1]


def draw_slot_request(key, part):
    return placement_tables(key)[0]


def draw_key_pool(key, part):
    normal_part = jnp.clip(jax.random.normal(key, (POOL_ALL, H * HD), jnp.float32), -6.0, 6.0)
    return normal_part.astype(jnp.bfloat16)


def level_of(key, dims, pieces, smallest, top_value):
    def one(axis_at, blocks):
        draws = jax.random.uniform(jax.random.fold_in(jax.random.fold_in(key, 6), axis_at), (blocks,), jnp.float32, smallest / len(pieces), top_value / len(pieces))
        return jnp.repeat(jnp.exp(draws), dims[axis_at] // blocks).reshape((-1,) + (1,) * (len(dims) - axis_at - 1))

    factor_of = one(*pieces[0])
    for cut in pieces[1:]:
        factor_of = factor_of * one(*cut)
    return factor_of


def normal_values(stream_key, shape, deviation, most, pieces=(), kind=jnp.bfloat16):
    entries = deviation * jax.random.normal(stream_key, shape, jnp.float32)
    if pieces:
        entries = entries * level_of(stream_key, shape, pieces, -0.22, 0.18)
    return jnp.clip(entries, -most, most).astype(kind)


def setup_inputs(seed: int = 0) -> dict:
    arg_keys = jax.random.split(jax.random.key(seed), 14)
    query_new = normal_values(arg_keys[0], (REQS, H * HD), 1.0, 6.0, ((0, 8), (1, 4)))
    key_new = normal_values(arg_keys[1], (REQS, H * HD), 1.0, 6.0, ((0, 8), (1, 4)))
    value_new = normal_values(arg_keys[2], (REQS, H * HD), 1.0, 6.0, ((0, 8), (1, 4)))
    key_pool = draw_key_pool(jax.random.fold_in(arg_keys[13], 71), 0)
    value_pool = normal_values(arg_keys[4], (POOL_ALL, H * HD), 1.0, 6.0, ((0, 8), (1, 4)))
    lengths = draw_lengths(jax.random.fold_in(arg_keys[13], 71), 0)
    slot_request = draw_slot_request(jax.random.fold_in(arg_keys[13], 71), 0)
    residual = normal_values(arg_keys[7], (REQS, D), 1.0, 6.0, ((1, 8),))
    out_proj = normal_values(arg_keys[8], (H * HD, D), (H * HD // 4) ** -0.5, 0.15625, ((0, 4), (1, 8)))
    norm_gain = jnp.clip(1.0 + 0.1 * jax.random.normal(arg_keys[9], (D,), jnp.float32), 0.5, 1.5).astype(jnp.bfloat16)
    gate_proj = normal_values(arg_keys[10], (D, FF), D ** -0.5, 0.078125, ((1, 32),))
    up_proj = normal_values(arg_keys[11], (D, FF), D ** -0.5, 0.078125, ((1, 32),))
    down_proj = normal_values(arg_keys[12], (FF, D), (FF // 16) ** -0.5, 0.21875, ((0, 8), (1, 4)))
    return dict(query_new=query_new, key_new=key_new, value_new=value_new, key_pool=key_pool, value_pool=value_pool, lengths=lengths, slot_request=slot_request, residual=residual, out_proj=out_proj, norm_gain=norm_gain, gate_proj=gate_proj, up_proj=up_proj, down_proj=down_proj)


def rope_tables(positions):
    half_dim = HD // 2
    freq_steps = jnp.arange(half_dim, dtype=jnp.float32)
    inverse = jnp.exp(freq_steps * (-2.0 * math.log(10000.0) / HD))
    angles = positions.astype(jnp.float32)[:, None] * inverse[None, :]
    return (jnp.cos(angles), jnp.sin(angles))

def rotate_half(vectors, cosine, sine_table):
    half_dim = HD // 2
    first_half = vectors[..., :half_dim]
    second = vectors[..., half_dim:]
    cos_grid = cosine[:, None, :]
    sin_grid = sine_table[:, None, :]
    return jnp.concatenate([first_half * cos_grid - second * sin_grid, second * cos_grid + first_half * sin_grid], axis=-1)

def attend(query_rot, key_rot, value_new, pool_keys, pool_values, seg_lengths):
    score_scale = HD ** (-0.5)
    seg_ends = jnp.cumsum(seg_lengths)
    starts = seg_ends - seg_lengths
    places = jnp.arange(pool_keys.shape[0], dtype=jnp.int32)
    member = (places[None, :] >= starts[:, None]) & (places[None, :] < seg_ends[:, None])
    scores = jnp.einsum('rgd,pgd->grp', query_rot.astype(jnp.float32), pool_keys.astype(jnp.float32)) * score_scale
    own_score = lax.optimization_barrier(jnp.sum(query_rot.astype(jnp.float32) * key_rot.astype(jnp.float32), axis=-1)).T * score_scale
    masked = jnp.where(member[None], scores, -jnp.inf)
    row_top = jnp.maximum(lax.optimization_barrier(jnp.max(masked, axis=-1)), own_score)
    weights = jnp.where(member[None], jnp.exp(scores - row_top[:, :, None]), 0.0)
    own_weight = jnp.exp(own_score - row_top)
    row_total = lax.optimization_barrier(jnp.sum(weights, axis=-1)) + own_weight
    weights_bf = lax.optimization_barrier(weights.astype(jnp.bfloat16)).astype(jnp.float32)
    own_bf = lax.optimization_barrier(own_weight.astype(jnp.bfloat16)).astype(jnp.float32)
    summed = jnp.einsum('grp,pgd->rgd', weights_bf, pool_values.astype(jnp.float32))
    summed = summed + own_bf.T[:, :, None] * value_new.astype(jnp.float32)
    return (summed / row_total.T[:, :, None]).astype(jnp.bfloat16)

def reference(query_new, key_new, value_new, key_pool, value_pool, lengths, slot_request, residual, out_proj, norm_gain, gate_proj, up_proj, down_proj):
    slot_length = jnp.take(lengths, slot_request, axis=0)
    cosine, sine_table = rope_tables(slot_length)
    shaped = (REQS, H, HD)
    query_rot = rotate_half(query_new.astype(jnp.float32).reshape(shaped), cosine, sine_table).astype(jnp.bfloat16)
    key_rot = rotate_half(key_new.astype(jnp.float32).reshape(shaped), cosine, sine_table).astype(jnp.bfloat16)
    values_new = value_new.reshape(shaped)

    def per_owner(owner):
        first_slot = (owner * REQ_DEV).astype(jnp.int32)
        first_row = (owner * POOL).astype(jnp.int32)
        pool_keys = lax.dynamic_slice_in_dim(key_pool, first_row, POOL, 0).reshape(POOL, H, HD)
        pool_values = lax.dynamic_slice_in_dim(value_pool, first_row, POOL, 0).reshape(POOL, H, HD)
        return attend(lax.dynamic_slice_in_dim(query_rot, first_slot, REQ_DEV, 0), lax.dynamic_slice_in_dim(key_rot, first_slot, REQ_DEV, 0), lax.dynamic_slice_in_dim(values_new, first_slot, REQ_DEV, 0), pool_keys, pool_values, lax.dynamic_slice_in_dim(slot_length, first_slot, REQ_DEV, 0))
    attention = lax.map(per_owner, jnp.arange(N_REQ, dtype=jnp.int32)).reshape(REQS, H * HD)
    projected = jnp.dot(attention, out_proj, preferred_element_type=jnp.float32)
    attended = (jnp.take(residual, slot_request, axis=0).astype(jnp.float32) + projected).astype(jnp.bfloat16)
    widened = attended.astype(jnp.float32)
    inverse = lax.rsqrt(lax.optimization_barrier(jnp.mean(widened * widened, axis=-1, keepdims=True)) + 1e-05)
    scaled = (widened * inverse * norm_gain.astype(jnp.float32)[None, :]).astype(jnp.bfloat16)
    gate_pre = jnp.dot(scaled, gate_proj, preferred_element_type=jnp.float32)
    upward = jnp.dot(scaled, up_proj, preferred_element_type=jnp.float32)
    active = (jax.nn.silu(gate_pre) * upward).astype(jnp.bfloat16)
    ffn_out = jnp.dot(active, down_proj, preferred_element_type=jnp.float32).astype(jnp.bfloat16)
    return (attended, ffn_out)
```

```python
import math

import jax
import jax.numpy as jnp
from jax import lax
from jax.experimental import pallas as pl
from jax.experimental.pallas import tpu as pltpu
from jax.sharding import PartitionSpec as P

D = 5120
HD = 128


def rope_tables(positions):
    half_dim = HD // 2
    freq_steps = jnp.arange(half_dim, dtype=jnp.float32)
    inverse = jnp.exp(freq_steps * (-2.0 * math.log(10000.0) / HD))
    angles = positions.astype(jnp.float32)[:, None] * inverse[None, :]
    return (jnp.cos(angles), jnp.sin(angles))


def swap_halves(v):
    half = HD // 2
    return jnp.concatenate([v[:, half:], v[:, :half]], axis=1)


def attend_kernel(q_ref, k_ref, v_ref, kp_ref, vp_ref, cos_ref, sin_ref, st_ref, en_ref, out_ref):
    scale = HD ** (-0.5)
    owned = q_ref.shape[0]
    rows = kp_ref.shape[0]
    cosine = cos_ref[...]
    sine = sin_ref[...]
    rotated = []
    own = []
    for j in range(2):
        cols = slice(j * HD, (j + 1) * HD)
        q = q_ref[:, cols].astype(jnp.float32)
        k = k_ref[:, cols].astype(jnp.float32)
        q = (q * cosine + swap_halves(q) * sine).astype(jnp.bfloat16)
        k = (k * cosine + swap_halves(k) * sine).astype(jnp.bfloat16)
        rotated.append(q)
        own.append(
            jnp.sum(q.astype(jnp.float32) * k.astype(jnp.float32), axis=-1, keepdims=True) * scale
        )
    blank = jnp.zeros((owned, HD), jnp.bfloat16)
    both = jnp.concatenate(
        [
            jnp.concatenate([rotated[0], blank], axis=1),
            jnp.concatenate([blank, rotated[1]], axis=1),
        ],
        axis=0,
    )
    own = jnp.concatenate(own, axis=0)
    scores = (
        lax.dot_general(
            both, kp_ref[...], (((1,), (1,)), ((), ())), preferred_element_type=jnp.float32
        )
        * scale
    )
    starts = jnp.concatenate([st_ref[...]] * 2, axis=0)
    ends = jnp.concatenate([en_ref[...]] * 2, axis=0)
    places = lax.broadcasted_iota(jnp.int32, (2 * owned, rows), 1)
    member = (places >= starts) & (places < ends)
    masked = jnp.where(member, scores, -jnp.inf)
    top = jnp.maximum(jnp.max(masked, axis=-1, keepdims=True), own)
    weights = jnp.exp(masked - top)
    own_weight = jnp.exp(own - top)
    total = jnp.sum(weights, axis=-1, keepdims=True) + own_weight
    summed = jnp.dot(
        weights.astype(jnp.bfloat16), vp_ref[...], preferred_element_type=jnp.float32
    )
    own_weight = own_weight.astype(jnp.bfloat16).astype(jnp.float32)
    for j in range(2):
        cols = slice(j * HD, (j + 1) * HD)
        part = slice(j * owned, (j + 1) * owned)
        value = v_ref[:, cols].astype(jnp.float32)
        out_ref[:, cols] = (
            (summed[part, cols] + own_weight[part] * value) / total[part]
        ).astype(jnp.bfloat16)


def attend_local(query_new, key_new, value_new, key_pool, value_pool, seg_lengths):
    owned, width = query_new.shape
    rows = key_pool.shape[0]
    cosine, sine = rope_tables(seg_lengths)
    cosine = jnp.concatenate([cosine, cosine], axis=1)
    sine = jnp.concatenate([-sine, sine], axis=1)
    ends = jnp.cumsum(seg_lengths)
    starts = ends - seg_lengths
    wide = 2 * HD
    slots = pl.BlockSpec((owned, wide), lambda i: (0, i))
    pool = pl.BlockSpec((rows, wide), lambda i: (0, i))
    table = pl.BlockSpec((owned, HD), lambda i: (0, 0))
    edge = pl.BlockSpec((owned, 1), lambda i: (0, 0))
    return pl.pallas_call(
        attend_kernel,
        grid=(width // wide,),
        in_specs=[slots, slots, slots, pool, pool, table, table, edge, edge],
        out_specs=slots,
        out_shape=jax.ShapeDtypeStruct((owned, width), jnp.bfloat16),
        compiler_params=pltpu.CompilerParams(vmem_limit_bytes=48 * 1024 * 1024),
        cost_estimate=pl.CostEstimate(
            flops=4 * owned * rows * width,
            bytes_accessed=4 * rows * width,
            transcendentals=owned * rows * width // HD,
        ),
    )(
        query_new,
        key_new,
        value_new,
        key_pool,
        value_pool,
        cosine,
        sine,
        starts[:, None],
        ends[:, None],
    )


def dot_turned(left, right):
    return lax.dot_general(
        left, right, (((1,), (1,)), ((), ())), preferred_element_type=jnp.float32
    )


def layer_kernel(
    att_ref,
    res_ref,
    gain_ref,
    out_hbm,
    gate_hbm,
    up_hbm,
    down_hbm,
    attended_ref,
    ffn_ref,
    wo,
    wg,
    wu,
    wd,
    att_all,
    part,
    core_out,
    core_in,
    y_out,
    y_in,
    hidden,
    squares,
    acc_gate,
    acc_up,
    active,
    down_part,
    x_out,
    x_in,
    z_out,
    z_in,
    w_sem,
    a_zs,
    a_zr,
    a_xs,
    a_xr,
    c_s,
    c_r,
    p_s,
    p_r,
    h_zs,
    h_zr,
    h_xs,
    h_xr,
    h_ys,
    h_yr,
    h_as,
    h_ar,
    h_bs,
    h_br,
    h_cs,
    h_cr,
    g_ys,
    g_yr,
    g_cs,
    g_cr,
    f_xs,
    f_xr,
    f_zs,
    f_zr,
):
    r = lax.axis_index("req")
    h = lax.axis_index("head")
    z = r // 2
    x = r % 2
    y = h // 2
    c = h % 2
    xn = 1 - x
    yn = 1 - y
    cn = 1 - c
    zs = [(z + k) % 4 for k in range(4)]
    to_x = (z * 2 + xn, h)
    to_y = (r, yn * 2 + c)
    to_c = (r, y * 2 + cn)
    to_z = [(zs[k] * 2 + x, h) for k in range(4)]
    f32 = jnp.float32
    bf16 = jnp.bfloat16
    sent = []

    def copy(src, dst, send_sem, recv_sem, device):
        return pltpu.make_async_remote_copy(
            src_ref=src,
            dst_ref=dst,
            send_sem=send_sem,
            recv_sem=recv_sem,
            device_id=device,
            device_id_type=pl.DeviceIdType.MESH,
        )

    def send(*args):
        one = copy(*args)
        one.start()
        sent.append(one)

    def arrived(dst, send_sem, recv_sem, device):
        copy(dst, dst, send_sem, recv_sem, device).wait_recv()

    loads = [
        pltpu.make_async_copy(src, dst, w_sem.at[i])
        for i, (src, dst) in enumerate(
            ((out_hbm, wo), (gate_hbm, wg), (up_hbm, wu), (down_hbm, wd))
        )
    ]
    for load in loads:
        load.start()

    barrier = pltpu.get_barrier_semaphore()
    for device in (to_z[1], to_z[2], to_z[3], to_x, to_y, to_c):
        pl.semaphore_signal(
            barrier, inc=1, device_id=device, device_id_type=pl.DeviceIdType.MESH
        )
    pl.semaphore_wait(barrier, 6)

    for k in (2, 1, 3):
        send(att_ref, att_all.at[r], a_zs.at[k], a_zr.at[z], to_z[k])
    send(att_ref, att_all.at[r], a_xs.at[z], a_xr.at[z], to_x)
    att_all[r] = att_ref[...]
    loads[0].wait()
    for k in (0, 1, 3, 2):
        q = zs[k]
        if k:
            mine = att_all.at[q * 2 + x]
            arrived(mine, a_zs.at[k], a_zr.at[q], to_z[k])
            send(mine, mine, a_xs.at[q], a_xr.at[q], to_x)
    for k in (0, 1, 3, 2):
        q = zs[k]
        arrived(att_all.at[q * 2 + xn], a_xs.at[q], a_xr.at[q], to_x)
        pair = att_all[pl.ds(q * 2, 2)].reshape(part.shape[1], att_ref.shape[1])
        part[q] = jnp.dot(pair, wo[...], preferred_element_type=f32)

    for qy in (yn, y):
        core_out[qy] = part[qy * 2 + cn].astype(bf16)
        send(core_out.at[qy], core_in.at[qy], c_s.at[qy], c_r.at[qy], to_c)
    arrived(core_in.at[yn], c_s.at[yn], c_r.at[yn], to_c)
    y_out[...] = (part[yn * 2 + c] + core_in[yn].astype(f32)).astype(bf16)
    send(y_out, y_in, p_s, p_r, to_y)
    arrived(core_in.at[y], c_s.at[y], c_r.at[y], to_c)
    total = part[h] + core_in[y].astype(f32) + res_ref[...].astype(f32)
    arrived(y_in, p_s, p_r, to_y)
    mine = (total + y_in[...].astype(f32)).astype(bf16)
    attended_ref[...] = mine
    quarter = mine.shape[0]
    half = quarter // 2
    hidden[r, pl.ds(h * quarter, quarter), :] = mine

    def chunk(q, cx, cy, cc):
        return hidden.at[q * 2 + cx, pl.ds((cy * 2 + cc) * quarter, quarter), :]

    def halved(q, cx, cy, cc, which):
        return hidden.at[
            q * 2 + cx, pl.ds((cy * 2 + cc) * quarter + which * half, half), :
        ]

    def to_core(block, q, i):
        send(block, block, h_cs.at[q * 5 + i], h_cr.at[q * 5 + i], to_c)

    def from_core(block, q, i):
        arrived(block, h_cs.at[q * 5 + i], h_cr.at[q * 5 + i], to_c)

    def spread(k):
        q = zs[k]
        block = chunk(q, x, y, c)
        if k:
            arrived(block, h_zs.at[k], h_zr.at[q], to_z[k])
        send(block, block, h_xs.at[q], h_xr.at[q], to_x)
        send(block, block, h_ys.at[q], h_yr.at[q], to_y)
        to_core(block, q, 0)

    def diagonal(k):
        q = zs[k]
        block = chunk(q, xn, y, c)
        arrived(block, h_xs.at[q], h_xr.at[q], to_x)
        piece = halved(q, xn, y, c, 1)
        send(piece, piece, h_bs.at[q], h_br.at[q], to_y)
        to_core(block, q, 1)
        block = chunk(q, x, yn, c)
        arrived(block, h_ys.at[q], h_yr.at[q], to_y)
        piece = halved(q, x, yn, c, 0)
        send(piece, piece, h_as.at[q], h_ar.at[q], to_x)
        to_core(block, q, 2)

    def finish(k):
        q = zs[k]
        piece = halved(q, xn, yn, c, 0)
        arrived(piece, h_as.at[q], h_ar.at[q], to_x)
        to_core(piece, q, 3)
        piece = halved(q, xn, yn, c, 1)
        arrived(piece, h_bs.at[q], h_br.at[q], to_y)
        to_core(piece, q, 4)

    def collect(k):
        q = zs[k]
        from_core(chunk(q, x, y, cn), q, 0)
        from_core(chunk(q, xn, y, cn), q, 1)
        from_core(chunk(q, x, yn, cn), q, 2)
        from_core(halved(q, xn, yn, cn, 0), q, 3)
        from_core(halved(q, xn, yn, cn, 1), q, 4)

    width = mine.shape[1]
    tall = 2 * quarter

    def multiply(k):
        q = zs[k]

        def step(i, carry):
            rows = pl.ds(pl.multiple_of(i * tall, tall), tall)
            gate = up = square = None
            for cx in range(2):
                at = q * 2 + cx
                wide = hidden[at, rows, :].astype(f32)
                power = wide * wide
                for j in range(width // 128):
                    one = power[:, j * 128 : (j + 1) * 128]
                    square = one if square is None else square + one
                scaled = (wide * gain_ref[at]).astype(bf16)
                depth = pl.ds(pl.multiple_of(at * width, width), width)
                one = dot_turned(scaled, wg[:, depth])
                gate = one if gate is None else gate + one
                one = dot_turned(scaled, wu[:, depth])
                up = one if up is None else up + one
            if k == first:
                acc_gate[rows, :] = gate
                acc_up[rows, :] = up
                squares[rows, :] = square
            else:
                acc_gate[rows, :] += gate
                acc_up[rows, :] += up
                squares[rows, :] += square
            return carry

        lax.fori_loop(0, hidden.shape[1] // tall, step, 0)

    own_chunk = chunk(z, x, y, c)
    for k in (2, 1, 3):
        send(own_chunk, own_chunk, h_zs.at[k], h_zr.at[z], to_z[k])
    order = (0, 1, 3, 2)
    first = order[0]
    spread(order[0])
    loads[1].wait()
    loads[2].wait()
    for i in range(4):
        if i < 3:
            spread(order[i + 1])
        diagonal(order[i])
        if i:
            collect(order[i - 1])
            multiply(order[i - 1])
        finish(order[i])
    collect(order[3])
    multiply(order[3])

    def rows_of(q):
        return pl.ds(pl.multiple_of(q * quarter, quarter), quarter)

    late = (1, 3, 2, 0)
    hy = yn * 2 + c
    hc = y * 2 + cn
    hd = yn * 2 + cn
    for k in late:
        q = zs[k]
        mean = jnp.sum(squares[rows_of(q), :], axis=-1, keepdims=True) / D
        inverse = lax.rsqrt(mean + 1e-05)
        gate = acc_gate[rows_of(q), :] * inverse
        up = acc_up[rows_of(q), :] * inverse
        active[h, q] = (gate / (1.0 + jnp.exp(-gate)) * up).astype(bf16)
        block = active.at[h, q]
        send(block, block, g_ys.at[q], g_yr.at[q], to_y)
        send(block, block, g_cs.at[q], g_cr.at[q], to_c)
    loads[3].wait()
    units = active.shape[3]

    def reduce_x(k):
        q = zs[k]
        arrived(x_in.at[q], f_xs.at[q], f_xr.at[q], to_x)
        total = down_part[q, x] + x_in[q].astype(f32)
        if k:
            z_out[q] = total.astype(bf16)
            send(z_out.at[q], z_in.at[z], f_zs.at[q], f_zr.at[z], to_z[k])
            return None
        return total

    for i, k in enumerate(late):
        q = zs[k]
        block = active.at[hy, q]
        arrived(block, g_ys.at[q], g_yr.at[q], to_y)
        send(block, block, g_cs.at[4 + q], g_cr.at[4 + q], to_c)
        arrived(active.at[hc, q], g_cs.at[q], g_cr.at[q], to_c)
        arrived(active.at[hd, q], g_cs.at[4 + q], g_cr.at[4 + q], to_c)
        total = None
        for g in range(4):
            one = jnp.dot(
                active[g, q], wd[g * units : (g + 1) * units, :], preferred_element_type=f32
            )
            total = one if total is None else total + one
        down_part[q] = total.reshape(down_part.shape[1:])
        x_out[q] = down_part[q, xn].astype(bf16)
        send(x_out.at[q], x_in.at[q], f_xs.at[q], f_xr.at[q], to_x)
        if i:
            reduce_x(late[i - 1])
    total = reduce_x(0)
    for k in (1, 3, 2):
        arrived(z_in.at[zs[k]], f_zs.at[zs[k]], f_zr.at[zs[k]], to_z[k])
        total = total + z_in[zs[k]].astype(f32)
    ffn_ref[...] = total.astype(bf16)
    for one in sent:
        one.wait_send()


def layer_local(attention, rows, out_proj, norm_gain, gate_proj, up_proj, down_proj):
    owned, feats = attention.shape
    quarter, width = rows.shape
    gate_proj = gate_proj.T
    up_proj = up_proj.T
    units, hid = gate_proj.shape
    deep, cols = down_proj.shape
    blocks = hid // width
    bf16 = jnp.bfloat16
    f32 = jnp.float32
    dma = pltpu.SemaphoreType.DMA
    vmem = pl.BlockSpec(memory_space=pltpu.VMEM)
    hbm = pl.BlockSpec(memory_space=pl.ANY)
    gain = norm_gain.astype(f32).reshape(blocks, 1, width)
    return pl.pallas_call(
        layer_kernel,
        out_shape=(
            jax.ShapeDtypeStruct((quarter, width), bf16),
            jax.ShapeDtypeStruct((owned, cols), bf16),
        ),
        in_specs=[vmem, vmem, vmem, hbm, hbm, hbm, hbm],
        out_specs=(vmem, vmem),
        scratch_shapes=[
            pltpu.VMEM(out_proj.shape, bf16),
            pltpu.VMEM(gate_proj.shape, bf16),
            pltpu.VMEM(up_proj.shape, bf16),
            pltpu.VMEM(down_proj.shape, bf16),
            pltpu.VMEM((8, owned, feats), bf16),
            pltpu.VMEM((4, quarter, width), f32),
            pltpu.VMEM((2, quarter, width), bf16),
            pltpu.VMEM((2, quarter, width), bf16),
            pltpu.VMEM((quarter, width), bf16),
            pltpu.VMEM((quarter, width), bf16),
            pltpu.VMEM((blocks, 4 * quarter, width), bf16),
            pltpu.VMEM((4 * quarter, 128), f32),
            pltpu.VMEM((4 * quarter, units), f32),
            pltpu.VMEM((4 * quarter, units), f32),
            pltpu.VMEM((4, 4, quarter, units), bf16),
            pltpu.VMEM((4, 2, owned, cols), f32),
            pltpu.VMEM((4, owned, cols), bf16),
            pltpu.VMEM((4, owned, cols), bf16),
            pltpu.VMEM((4, owned, cols), bf16),
            pltpu.VMEM((4, owned, cols), bf16),
            dma((4,)),
            dma((4,)),
            dma((4,)),
            dma((4,)),
            dma((4,)),
            dma((2,)),
            dma((2,)),
            dma,
            dma,
            dma((4,)),
            dma((4,)),
            dma((4,)),
            dma((4,)),
            dma((4,)),
            dma((4,)),
            dma((4,)),
            dma((4,)),
            dma((4,)),
            dma((4,)),
            dma((20,)),
            dma((20,)),
            dma((4,)),
            dma((4,)),
            dma((8,)),
            dma((8,)),
            dma((4,)),
            dma((4,)),
            dma((4,)),
            dma((4,)),
        ],
        compiler_params=pltpu.CompilerParams(
            collective_id=1, has_side_effects=True, vmem_limit_bytes=58 * 1024 * 1024
        ),
        cost_estimate=pl.CostEstimate(
            flops=2 * 4 * quarter * (2 * hid * units + deep * cols + feats * width),
            bytes_accessed=2 * (2 * hid * units + deep * cols + feats * width),
            transcendentals=4 * quarter * units,
        ),
    )(attention, rows, gain, out_proj, gate_proj, up_proj, down_proj)


def body(
    query_new,
    key_new,
    value_new,
    key_pool,
    value_pool,
    lengths,
    slot_request,
    residual,
    out_proj,
    norm_gain,
    gate_proj,
    up_proj,
    down_proj,
):
    owned = query_new.shape[0]
    req_count = lax.axis_size("req")
    head_count = lax.axis_size("head")
    first_slot = lax.axis_index("req") * owned
    my_requests = lax.dynamic_slice_in_dim(slot_request, first_slot, owned, 0)
    my_lengths = jnp.take(lengths, my_requests, axis=0)
    attention = attend_local(query_new, key_new, value_new, key_pool, value_pool, my_lengths)
    if (req_count, head_count) == (8, 4):
        quarter = slot_request.shape[0] // head_count
        quarter_slots = lax.dynamic_slice_in_dim(
            slot_request, lax.axis_index("head") * quarter, quarter, 0
        )
        return layer_local(
            attention,
            jnp.take(residual, quarter_slots, axis=0),
            out_proj,
            norm_gain,
            gate_proj,
            up_proj,
            down_proj,
        )
    partial_sums = jnp.dot(
        lax.all_gather(attention, "req", axis=0, tiled=True),
        out_proj,
        preferred_element_type=jnp.float32,
    )
    summed = lax.psum_scatter(partial_sums, "head", scatter_dimension=0, tiled=True)
    quarter = summed.shape[0]
    quarter_slots = lax.dynamic_slice_in_dim(
        slot_request, lax.axis_index("head") * quarter, quarter, 0
    )
    attended = (jnp.take(residual, quarter_slots, axis=0).astype(jnp.float32) + summed).astype(
        jnp.bfloat16
    )
    column_width = attended.shape[1]
    gain_grid = norm_gain.astype(jnp.float32).reshape(req_count, 1, column_width)
    everywhere = lax.all_gather(attended[None], ("req", "head"), axis=0, tiled=True)
    hidden_grid = everywhere.reshape(req_count, head_count, quarter, column_width).astype(
        jnp.float32
    )
    squares = jnp.sum(hidden_grid * hidden_grid, axis=(0, 3))
    inverse = lax.rsqrt(squares / D + 1e-05)
    scaled = (hidden_grid * inverse[None, :, :, None] * gain_grid[:, None]).astype(jnp.bfloat16)
    col_block = gate_proj.shape[1]
    gate_pre = jnp.einsum(
        "rhbc,rcf->hbf",
        scaled,
        gate_proj.reshape(req_count, column_width, col_block),
        preferred_element_type=jnp.float32,
    )
    upward = jnp.einsum(
        "rhbc,rcf->hbf",
        scaled,
        up_proj.reshape(req_count, column_width, col_block),
        preferred_element_type=jnp.float32,
    )
    active = (jax.nn.silu(gate_pre) * upward).astype(jnp.bfloat16)
    gathered = lax.all_gather(active, "head", axis=2, tiled=True)
    active_all = gathered.reshape(head_count * quarter, head_count * col_block)
    ffn_out = lax.psum_scatter(
        jnp.dot(active_all, down_proj, preferred_element_type=jnp.float32).astype(jnp.bfloat16),
        "req",
        scatter_dimension=0,
        tiled=True,
    )
    return (attended, ffn_out)


def solution(mesh):
    placed = (
        P("req", "head"),
        P("req", "head"),
        P("req", "head"),
        P("req", "head"),
        P("req", "head"),
        P(),
        P(),
        P(None, "req"),
        P("head", "req"),
        P(),
        P(None, ("req", "head")),
        P(None, ("req", "head")),
        P("req", "head"),
    )
    return jax.shard_map(
        body,
        mesh=mesh,
        in_specs=placed,
        out_specs=(P("head", "req"), P("req", "head")),
        check_vma=False,
    )
```

```python
import math

import jax
import jax.numpy as jnp
from jax import lax
from jax.experimental import pallas as pl
from jax.experimental.pallas import tpu as pltpu
from jax.sharding import PartitionSpec as P

D = 5120
HD = 128


def rope_tables(positions):
    half_dim = HD // 2
    freq_steps = jnp.arange(half_dim, dtype=jnp.float32)
    inverse = jnp.exp(freq_steps * (-2.0 * math.log(10000.0) / HD))
    angles = positions.astype(jnp.float32)[:, None] * inverse[None, :]
    return (jnp.cos(angles), jnp.sin(angles))


def dot_turned(left, right):
    return lax.dot_general(
        left, right, (((1,), (1,)), ((), ())), preferred_element_type=jnp.float32
    )


def swap_halves(v):
    half = HD // 2
    return jnp.concatenate([v[:, half:], v[:, :half]], axis=1)


def attend_pair(q_pair, k_pair, v_pair, key_rows, value_rows, cosine, sine, starts, ends):
    scale = HD ** (-0.5)
    owned = q_pair.shape[0]
    rows = key_rows.shape[0]
    rotated = []
    own = []
    for j in range(2):
        cols = slice(j * HD, (j + 1) * HD)
        q = q_pair[:, cols].astype(jnp.float32)
        k = k_pair[:, cols].astype(jnp.float32)
        q = (q * cosine + swap_halves(q) * sine).astype(jnp.bfloat16)
        k = (k * cosine + swap_halves(k) * sine).astype(jnp.bfloat16)
        rotated.append(q)
        own.append(
            jnp.sum(q.astype(jnp.float32) * k.astype(jnp.float32), axis=-1, keepdims=True) * scale
        )
    blank = jnp.zeros((owned, HD), jnp.bfloat16)
    both = jnp.concatenate(
        [
            jnp.concatenate([rotated[0], blank], axis=1),
            jnp.concatenate([blank, rotated[1]], axis=1),
        ],
        axis=0,
    )
    own = jnp.concatenate(own, axis=0)
    scores = dot_turned(both, key_rows) * scale
    starts = jnp.concatenate([starts] * 2, axis=0)
    ends = jnp.concatenate([ends] * 2, axis=0)
    places = lax.broadcasted_iota(jnp.int32, (2 * owned, rows), 1)
    member = (places >= starts) & (places < ends)
    masked = jnp.where(member, scores, -jnp.inf)
    top = jnp.maximum(jnp.max(masked, axis=-1, keepdims=True), own)
    weights = jnp.exp(masked - top)
    own_weight = jnp.exp(own - top)
    total = jnp.sum(weights, axis=-1, keepdims=True) + own_weight
    summed = jnp.dot(weights.astype(jnp.bfloat16), value_rows, preferred_element_type=jnp.float32)
    own_weight = own_weight.astype(jnp.bfloat16).astype(jnp.float32)
    heads = []
    for j in range(2):
        cols = slice(j * HD, (j + 1) * HD)
        part = slice(j * owned, (j + 1) * owned)
        value = v_pair[:, cols].astype(jnp.float32)
        heads.append((summed[part, cols] + own_weight[part] * value) / total[part])
    return jnp.concatenate(heads, axis=1).astype(jnp.bfloat16)


def attend_kernel(q_ref, k_ref, v_ref, kp_ref, vp_ref, cos_ref, sin_ref, st_ref, en_ref, out_ref):
    out_ref[...] = attend_pair(
        q_ref[...],
        k_ref[...],
        v_ref[...],
        kp_ref[...],
        vp_ref[...],
        cos_ref[...],
        sin_ref[...],
        st_ref[...],
        en_ref[...],
    )


def pick(table_row, chosen):
    places = lax.broadcasted_iota(jnp.int32, (chosen.shape[0], table_row.shape[1]), 1)
    hit = places.astype(jnp.float32) == chosen
    return jnp.sum(jnp.where(hit, table_row, 0.0), axis=1, keepdims=True)


def as_column(row):
    count = row.shape[1]
    down = lax.broadcasted_iota(jnp.int32, (count, count), 0)
    across = lax.broadcasted_iota(jnp.int32, (count, count), 1)
    return jnp.sum(jnp.where(down == across, row, 0.0), axis=1, keepdims=True)


def running_starts(column):
    count = column.shape[0]
    down = lax.broadcasted_iota(jnp.int32, (count, count), 0)
    across = lax.broadcasted_iota(jnp.int32, (count, count), 1)
    row = jnp.sum(jnp.where(down == across, column, 0.0), axis=0, keepdims=True)
    return jnp.sum(jnp.where(across < down, row, 0.0), axis=1, keepdims=True)


def attend_local(query_new, key_new, value_new, key_pool, value_pool, seg_lengths):
    owned, width = query_new.shape
    rows = key_pool.shape[0]
    cosine, sine = rope_tables(seg_lengths)
    cosine = jnp.concatenate([cosine, cosine], axis=1)
    sine = jnp.concatenate([-sine, sine], axis=1)
    ends = jnp.cumsum(seg_lengths)
    starts = ends - seg_lengths
    wide = 2 * HD
    slots = pl.BlockSpec((owned, wide), lambda i: (0, i))
    pool = pl.BlockSpec((rows, wide), lambda i: (0, i))
    table = pl.BlockSpec((owned, HD), lambda i: (0, 0))
    edge = pl.BlockSpec((owned, 1), lambda i: (0, 0))
    return pl.pallas_call(
        attend_kernel,
        grid=(width // wide,),
        in_specs=[slots, slots, slots, pool, pool, table, table, edge, edge],
        out_specs=slots,
        out_shape=jax.ShapeDtypeStruct((owned, width), jnp.bfloat16),
        compiler_params=pltpu.CompilerParams(vmem_limit_bytes=48 * 1024 * 1024),
        cost_estimate=pl.CostEstimate(
            flops=4 * owned * rows * width,
            bytes_accessed=4 * rows * width,
            transcendentals=owned * rows * width // HD,
        ),
    )(
        query_new,
        key_new,
        value_new,
        key_pool,
        value_pool,
        cosine,
        sine,
        starts[:, None],
        ends[:, None],
    )


def layer_kernel(
    length_ref,
    slot_ref,
    gain_ref,
    q_hbm,
    k_hbm,
    v_hbm,
    kp_hbm,
    vp_hbm,
    res_hbm,
    out_hbm,
    gate_hbm,
    up_hbm,
    down_hbm,
    attended_ref,
    ffn_ref,
    wo,
    wg,
    wu,
    wd,
    q_in,
    k_in,
    v_in,
    kp_in,
    vp_in,
    res_in,
    att_all,
    part,
    core_out,
    core_in,
    y_out,
    y_in,
    hidden,
    squares,
    acc_gate,
    acc_up,
    active,
    down_part,
    x_out,
    x_in,
    z_out,
    z_in,
    cos_tab,
    sin_tab,
    edge_tab,
    res_rows,
    n_sem,
    kp_sem,
    vp_sem,
    w_sem,
    a_zs,
    a_zr,
    a_xs,
    a_xr,
    c_s,
    c_r,
    p_s,
    p_r,
    h_zs,
    h_zr,
    h_xs,
    h_xr,
    h_ys,
    h_yr,
    h_as,
    h_ar,
    h_bs,
    h_br,
    h_cs,
    h_cr,
    g_ys,
    g_yr,
    g_cs,
    g_cr,
    f_xs,
    f_xr,
    f_zs,
    f_zr,
):
    r = lax.axis_index("req")
    h = lax.axis_index("head")
    z = r // 2
    x = r % 2
    y = h // 2
    c = h % 2
    xn = 1 - x
    yn = 1 - y
    cn = 1 - c
    zs = [(z + k) % 4 for k in range(4)]
    to_x = (z * 2 + xn, h)
    to_y = (r, yn * 2 + c)
    to_c = (r, y * 2 + cn)
    to_z = [(zs[k] * 2 + x, h) for k in range(4)]
    f32 = jnp.float32
    bf16 = jnp.bfloat16
    sent = []

    def copy(src, dst, send_sem, recv_sem, device):
        return pltpu.make_async_remote_copy(
            src_ref=src,
            dst_ref=dst,
            send_sem=send_sem,
            recv_sem=recv_sem,
            device_id=device,
            device_id_type=pl.DeviceIdType.MESH,
        )

    def send(*args):
        one = copy(*args)
        one.start()
        sent.append(one)

    def arrived(dst, send_sem, recv_sem, device):
        copy(dst, dst, send_sem, recv_sem, device).wait_recv()

    wide = att_all.shape[3]
    pieces = att_all.shape[0]

    def pair_cols(j):
        return pl.ds(pl.multiple_of(j * wide, wide), wide)

    def pool_loads(j):
        slot = j % 2
        return (
            pltpu.make_async_copy(kp_hbm.at[:, pair_cols(j)], kp_in.at[slot], kp_sem.at[slot]),
            pltpu.make_async_copy(vp_hbm.at[:, pair_cols(j)], vp_in.at[slot], vp_sem.at[slot]),
        )

    new_loads = [
        pltpu.make_async_copy(src, dst, n_sem.at[i])
        for i, (src, dst) in enumerate(((q_hbm, q_in), (k_hbm, k_in), (v_hbm, v_in)))
    ]
    loads = [
        pltpu.make_async_copy(src, dst, w_sem.at[i])
        for i, (src, dst) in enumerate(
            ((out_hbm, wo), (gate_hbm, wg), (up_hbm, wu), (down_hbm, wd), (res_hbm, res_in))
        )
    ]
    barrier = pltpu.get_barrier_semaphore()
    for device in (to_z[1], to_z[2], to_z[3], to_x, to_y, to_c):
        pl.semaphore_signal(
            barrier, inc=1, device_id=device, device_id_type=pl.DeviceIdType.MESH
        )
    for load in new_loads:
        load.start()
    for j in range(2):
        for load in pool_loads(j):
            load.start()
    for load in (loads[0], loads[4], loads[1], loads[2], loads[3]):
        load.start()

    length_row = length_ref[...].astype(f32)
    owned = q_in.shape[0]
    slot_len = pick(length_row, as_column(slot_ref[pl.ds(r, 1), :].astype(f32)))
    begin = running_starts(slot_len)
    starts = begin.astype(jnp.int32)
    ends = (begin + slot_len).astype(jnp.int32)
    lane = lax.broadcasted_iota(jnp.int32, (1, HD), 1)
    freq = (lane % (HD // 2)).astype(f32)
    angles = slot_len * jnp.exp(freq * (-2.0 * math.log(10000.0) / HD))
    cosine = jnp.cos(angles)
    sine = jnp.where(lane < HD // 2, -1.0, 1.0) * jnp.sin(angles)
    cos_tab[...] = cosine
    sin_tab[...] = sine
    edge_tab[0] = jnp.broadcast_to(starts, (owned, HD))
    edge_tab[1] = jnp.broadcast_to(ends, (owned, HD))
    part[...] = jnp.zeros_like(part)
    for load in new_loads:
        load.wait()
    pl.semaphore_wait(barrier, 6)

    def attention_step(j, carry):
        @pl.when(j < pieces)
        def _():
            for load in pool_loads(j):
                load.wait()
            slot = j % 2
            att_all[j, r] = attend_pair(
                q_in[:, pair_cols(j)],
                k_in[:, pair_cols(j)],
                v_in[:, pair_cols(j)],
                kp_in[slot],
                vp_in[slot],
                cos_tab[...],
                sin_tab[...],
                edge_tab[0][:, :1],
                edge_tab[1][:, :1],
            )

            @pl.when(j + 2 < pieces)
            def _():
                for load in pool_loads(j + 2):
                    load.start()

            mine = att_all.at[j, r]
            for k in (1, 3, 2):
                copy(mine, mine, a_zs.at[j * 4 + k], a_zr.at[j * 4 + z], to_z[k]).start()
            copy(mine, mine, a_xs.at[j * 4 + z], a_xr.at[j * 4 + z], to_x).start()

        @pl.when((j >= 1) & (j < pieces + 1))
        def _():
            p = j - 1
            for k in (1, 3, 2):
                q = zs[k]
                mine = att_all.at[p, q * 2 + x]
                arrived(mine, a_zs.at[p * 4 + k], a_zr.at[p * 4 + q], to_z[k])
                copy(mine, mine, a_xs.at[p * 4 + q], a_xr.at[p * 4 + q], to_x).start()

        @pl.when(j >= 2)
        def _():
            p = j - 2
            for k in (0, 1, 3, 2):
                q = zs[k]
                arrived(
                    att_all.at[p, q * 2 + xn], a_xs.at[p * 4 + q], a_xr.at[p * 4 + q], to_x
                )
            every = att_all[p].reshape(4 * part.shape[1], wide)
            depth = pl.ds(pl.multiple_of(p * wide, wide), wide)
            part[...] += jnp.dot(every, wo[depth, :], preferred_element_type=f32).reshape(
                part.shape
            )

        return carry

    loads[0].wait()
    loads[4].wait()
    for i in range(2):
        chosen = as_column(slot_ref[pl.ds(h * 2 + i, 1), :].astype(f32))
        places = lax.broadcasted_iota(jnp.int32, (owned, res_in.shape[0]), 1).astype(f32)
        hit = jnp.where(places == chosen, 1.0, 0.0).astype(bf16)
        picked = jnp.dot(hit, res_in[...], preferred_element_type=f32)
        res_rows[i * owned : (i + 1) * owned, :] = picked
    lax.fori_loop(0, pieces + 2, attention_step, 0)

    for qy in (yn, y):
        core_out[qy] = part[qy * 2 + cn].astype(bf16)
        send(core_out.at[qy], core_in.at[qy], c_s.at[qy], c_r.at[qy], to_c)
    arrived(core_in.at[yn], c_s.at[yn], c_r.at[yn], to_c)
    y_out[...] = (part[yn * 2 + c] + core_in[yn].astype(f32)).astype(bf16)
    send(y_out, y_in, p_s, p_r, to_y)
    arrived(core_in.at[y], c_s.at[y], c_r.at[y], to_c)
    total = part[h] + core_in[y].astype(f32) + res_rows[...]
    arrived(y_in, p_s, p_r, to_y)
    mine = (total + y_in[...].astype(f32)).astype(bf16)
    attended_ref[...] = mine
    quarter = mine.shape[0]
    half = quarter // 2
    hidden[r, pl.ds(h * quarter, quarter), :] = mine

    def chunk(q, cx, cy, cc):
        return hidden.at[q * 2 + cx, pl.ds((cy * 2 + cc) * quarter, quarter), :]

    def halved(q, cx, cy, cc, which):
        return hidden.at[
            q * 2 + cx, pl.ds((cy * 2 + cc) * quarter + which * half, half), :
        ]

    def to_core(block, q, i):
        send(block, block, h_cs.at[q * 5 + i], h_cr.at[q * 5 + i], to_c)

    def from_core(block, q, i):
        arrived(block, h_cs.at[q * 5 + i], h_cr.at[q * 5 + i], to_c)

    def spread(k):
        q = zs[k]
        block = chunk(q, x, y, c)
        if k:
            arrived(block, h_zs.at[k], h_zr.at[q], to_z[k])
        send(block, block, h_xs.at[q], h_xr.at[q], to_x)
        send(block, block, h_ys.at[q], h_yr.at[q], to_y)
        to_core(block, q, 0)

    def diagonal(k):
        q = zs[k]
        block = chunk(q, xn, y, c)
        arrived(block, h_xs.at[q], h_xr.at[q], to_x)
        piece = halved(q, xn, y, c, 1)
        send(piece, piece, h_bs.at[q], h_br.at[q], to_y)
        to_core(block, q, 1)
        block = chunk(q, x, yn, c)
        arrived(block, h_ys.at[q], h_yr.at[q], to_y)
        piece = halved(q, x, yn, c, 0)
        send(piece, piece, h_as.at[q], h_ar.at[q], to_x)
        to_core(block, q, 2)

    def finish(k):
        q = zs[k]
        piece = halved(q, xn, yn, c, 0)
        arrived(piece, h_as.at[q], h_ar.at[q], to_x)
        to_core(piece, q, 3)
        piece = halved(q, xn, yn, c, 1)
        arrived(piece, h_bs.at[q], h_br.at[q], to_y)
        to_core(piece, q, 4)

    def collect(k):
        q = zs[k]
        from_core(chunk(q, x, y, cn), q, 0)
        from_core(chunk(q, xn, y, cn), q, 1)
        from_core(chunk(q, x, yn, cn), q, 2)
        from_core(halved(q, xn, yn, cn, 0), q, 3)
        from_core(halved(q, xn, yn, cn, 1), q, 4)

    width = mine.shape[1]
    tall = 2 * quarter

    def multiply(k):
        q = zs[k]

        def step(i, carry):
            rows = pl.ds(pl.multiple_of(i * tall, tall), tall)
            gate = up = square = None
            for cx in range(2):
                at = q * 2 + cx
                broad = hidden[at, rows, :].astype(f32)
                power = broad * broad
                for j in range(width // 128):
                    one = power[:, j * 128 : (j + 1) * 128]
                    square = one if square is None else square + one
                scaled = (broad * gain_ref[:, pl.ds(pl.multiple_of(at * width, width), width)].astype(f32)).astype(bf16)
                depth = pl.ds(pl.multiple_of(at * width, width), width)
                one = dot_turned(scaled, wg[:, depth])
                gate = one if gate is None else gate + one
                one = dot_turned(scaled, wu[:, depth])
                up = one if up is None else up + one
            if k == first:
                acc_gate[rows, :] = gate
                acc_up[rows, :] = up
                squares[rows, :] = square
            else:
                acc_gate[rows, :] += gate
                acc_up[rows, :] += up
                squares[rows, :] += square
            return carry

        lax.fori_loop(0, hidden.shape[1] // tall, step, 0)

    own_chunk = chunk(z, x, y, c)
    for k in (1, 3, 2):
        send(own_chunk, own_chunk, h_zs.at[k], h_zr.at[z], to_z[k])
    order = (0, 1, 3, 2)
    first = order[0]
    spread(order[0])
    loads[1].wait()
    loads[2].wait()
    for i in range(4):
        if i < 3:
            spread(order[i + 1])
        diagonal(order[i])
        if i:
            collect(order[i - 1])
            multiply(order[i - 1])
        finish(order[i])
    collect(order[3])
    multiply(order[3])

    def rows_of(q):
        return pl.ds(pl.multiple_of(q * quarter, quarter), quarter)

    late = (1, 3, 2, 0)
    hy = yn * 2 + c
    hc = y * 2 + cn
    hd = yn * 2 + cn
    for k in late:
        q = zs[k]
        mean = jnp.sum(squares[rows_of(q), :], axis=-1, keepdims=True) / D
        inverse = lax.rsqrt(mean + 1e-05)
        gate = acc_gate[rows_of(q), :] * inverse
        up = acc_up[rows_of(q), :] * inverse
        active[h, q] = (gate / (1.0 + jnp.exp(-gate)) * up).astype(bf16)
        block = active.at[h, q]
        send(block, block, g_ys.at[q], g_yr.at[q], to_y)
        send(block, block, g_cs.at[q], g_cr.at[q], to_c)
    loads[3].wait()
    units = active.shape[3]

    def reduce_x(k):
        q = zs[k]
        arrived(x_in.at[q], f_xs.at[q], f_xr.at[q], to_x)
        total = down_part[q, x] + x_in[q].astype(f32)
        if k:
            z_out[q] = total.astype(bf16)
            send(z_out.at[q], z_in.at[z], f_zs.at[q], f_zr.at[z], to_z[k])
            return None
        return total

    for i, k in enumerate(late):
        q = zs[k]
        block = active.at[hy, q]
        arrived(block, g_ys.at[q], g_yr.at[q], to_y)
        send(block, block, g_cs.at[4 + q], g_cr.at[4 + q], to_c)
        arrived(active.at[hc, q], g_cs.at[q], g_cr.at[q], to_c)
        arrived(active.at[hd, q], g_cs.at[4 + q], g_cr.at[4 + q], to_c)
        total = None
        for g in range(4):
            one = jnp.dot(
                active[g, q], wd[g * units : (g + 1) * units, :], preferred_element_type=f32
            )
            total = one if total is None else total + one
        down_part[q] = total.reshape(down_part.shape[1:])
        x_out[q] = down_part[q, xn].astype(bf16)
        send(x_out.at[q], x_in.at[q], f_xs.at[q], f_xr.at[q], to_x)
        if i:
            reduce_x(late[i - 1])
    total = reduce_x(0)
    for k in (1, 3, 2):
        arrived(z_in.at[zs[k]], f_zs.at[zs[k]], f_zr.at[zs[k]], to_z[k])
        total = total + z_in[zs[k]].astype(f32)
    ffn_ref[...] = total.astype(bf16)
    for one in sent:
        one.wait_send()

    def drain(j, carry):
        mine = att_all.at[j, r]
        for k in (1, 3, 2):
            copy(mine, mine, a_zs.at[j * 4 + k], a_zr.at[j * 4 + z], to_z[k]).wait_send()
        for k in range(4):
            q = zs[k]
            mine = att_all.at[j, q * 2 + x]
            copy(mine, mine, a_xs.at[j * 4 + q], a_xr.at[j * 4 + q], to_x).wait_send()
        return carry

    lax.fori_loop(0, pieces, drain, 0)


def layer_local(
    query_new,
    key_new,
    value_new,
    key_pool,
    value_pool,
    lengths,
    slot_request,
    residual,
    out_proj,
    norm_gain,
    gate_proj,
    up_proj,
    down_proj,
):
    owned, feats = query_new.shape
    rows = key_pool.shape[0]
    slots, width = residual.shape
    quarter = slots // 4
    wide = 2 * HD
    gate_proj = gate_proj.T
    up_proj = up_proj.T
    units, hid = gate_proj.shape
    deep, cols = down_proj.shape
    blocks = hid // width
    bf16 = jnp.bfloat16
    f32 = jnp.float32
    dma = pltpu.SemaphoreType.DMA
    vmem = pl.BlockSpec(memory_space=pltpu.VMEM)
    hbm = pl.BlockSpec(memory_space=pl.ANY)
    return pl.pallas_call(
        layer_kernel,
        out_shape=(
            jax.ShapeDtypeStruct((quarter, width), bf16),
            jax.ShapeDtypeStruct((owned, cols), bf16),
        ),
        in_specs=[vmem] * 3 + [hbm] * 10,
        out_specs=(vmem, vmem),
        scratch_shapes=[
            pltpu.VMEM(out_proj.shape, bf16),
            pltpu.VMEM(gate_proj.shape, bf16),
            pltpu.VMEM(up_proj.shape, bf16),
            pltpu.VMEM(down_proj.shape, bf16),
            pltpu.VMEM((owned, feats), bf16),
            pltpu.VMEM((owned, feats), bf16),
            pltpu.VMEM((owned, feats), bf16),
            pltpu.VMEM((2, rows, wide), bf16),
            pltpu.VMEM((2, rows, wide), bf16),
            pltpu.VMEM(residual.shape, bf16),
            pltpu.VMEM((feats // wide, 8, owned, wide), bf16),
            pltpu.VMEM((4, quarter, width), f32),
            pltpu.VMEM((2, quarter, width), bf16),
            pltpu.VMEM((2, quarter, width), bf16),
            pltpu.VMEM((quarter, width), bf16),
            pltpu.VMEM((quarter, width), bf16),
            pltpu.VMEM((blocks, 4 * quarter, width), bf16),
            pltpu.VMEM((4 * quarter, 128), f32),
            pltpu.VMEM((4 * quarter, units), f32),
            pltpu.VMEM((4 * quarter, units), f32),
            pltpu.VMEM((4, 4, quarter, units), bf16),
            pltpu.VMEM((4, 2, owned, cols), f32),
            pltpu.VMEM((4, owned, cols), bf16),
            pltpu.VMEM((4, owned, cols), bf16),
            pltpu.VMEM((4, owned, cols), bf16),
            pltpu.VMEM((4, owned, cols), bf16),
            pltpu.VMEM((owned, HD), f32),
            pltpu.VMEM((owned, HD), f32),
            pltpu.VMEM((2, owned, HD), jnp.int32),
            pltpu.VMEM((quarter, width), f32),
            dma((3,)),
            dma((2,)),
            dma((2,)),
            dma((5,)),
            dma((feats // wide * 4,)),
            dma((feats // wide * 4,)),
            dma((feats // wide * 4,)),
            dma((feats // wide * 4,)),
            dma((2,)),
            dma((2,)),
            dma,
            dma,
            dma((4,)),
            dma((4,)),
            dma((4,)),
            dma((4,)),
            dma((4,)),
            dma((4,)),
            dma((4,)),
            dma((4,)),
            dma((4,)),
            dma((4,)),
            dma((20,)),
            dma((20,)),
            dma((4,)),
            dma((4,)),
            dma((8,)),
            dma((8,)),
            dma((4,)),
            dma((4,)),
            dma((4,)),
            dma((4,)),
        ],
        compiler_params=pltpu.CompilerParams(
            collective_id=1, has_side_effects=True, vmem_limit_bytes=58 * 1024 * 1024
        ),
        cost_estimate=pl.CostEstimate(
            flops=2 * 4 * quarter * (2 * hid * units + deep * cols + feats * width),
            bytes_accessed=2 * (2 * hid * units + deep * cols + feats * width),
            transcendentals=4 * quarter * units,
        ),
    )(
        lengths.reshape(1, slots),
        slot_request.reshape(slots // owned, owned),
        norm_gain.reshape(1, hid),
        query_new,
        key_new,
        value_new,
        key_pool,
        value_pool,
        residual,
        out_proj,
        gate_proj,
        up_proj,
        down_proj,
    )


def body(
    query_new,
    key_new,
    value_new,
    key_pool,
    value_pool,
    lengths,
    slot_request,
    residual,
    out_proj,
    norm_gain,
    gate_proj,
    up_proj,
    down_proj,
):
    owned = query_new.shape[0]
    req_count = lax.axis_size("req")
    head_count = lax.axis_size("head")
    if (req_count, head_count) == (8, 4):
        return layer_local(
            query_new,
            key_new,
            value_new,
            key_pool,
            value_pool,
            lengths,
            slot_request,
            residual,
            out_proj,
            norm_gain,
            gate_proj,
            up_proj,
            down_proj,
        )
    first_slot = lax.axis_index("req") * owned
    my_requests = lax.dynamic_slice_in_dim(slot_request, first_slot, owned, 0)
    my_lengths = jnp.take(lengths, my_requests, axis=0)
    attention = attend_local(query_new, key_new, value_new, key_pool, value_pool, my_lengths)
    partial_sums = jnp.dot(
        lax.all_gather(attention, "req", axis=0, tiled=True),
        out_proj,
        preferred_element_type=jnp.float32,
    )
    summed = lax.psum_scatter(partial_sums, "head", scatter_dimension=0, tiled=True)
    quarter = summed.shape[0]
    quarter_slots = lax.dynamic_slice_in_dim(
        slot_request, lax.axis_index("head") * quarter, quarter, 0
    )
    attended = (jnp.take(residual, quarter_slots, axis=0).astype(jnp.float32) + summed).astype(
        jnp.bfloat16
    )
    column_width = attended.shape[1]
    gain_grid = norm_gain.astype(jnp.float32).reshape(req_count, 1, column_width)
    everywhere = lax.all_gather(attended[None], ("req", "head"), axis=0, tiled=True)
    hidden_grid = everywhere.reshape(req_count, head_count, quarter, column_width).astype(
        jnp.float32
    )
    squares = jnp.sum(hidden_grid * hidden_grid, axis=(0, 3))
    inverse = lax.rsqrt(squares / D + 1e-05)
    scaled = (hidden_grid * inverse[None, :, :, None] * gain_grid[:, None]).astype(jnp.bfloat16)
    col_block = gate_proj.shape[1]
    gate_pre = jnp.einsum(
        "rhbc,rcf->hbf",
        scaled,
        gate_proj.reshape(req_count, column_width, col_block),
        preferred_element_type=jnp.float32,
    )
    upward = jnp.einsum(
        "rhbc,rcf->hbf",
        scaled,
        up_proj.reshape(req_count, column_width, col_block),
        preferred_element_type=jnp.float32,
    )
    active = (jax.nn.silu(gate_pre) * upward).astype(jnp.bfloat16)
    gathered = lax.all_gather(active, "head", axis=2, tiled=True)
    active_all = gathered.reshape(head_count * quarter, head_count * col_block)
    ffn_out = lax.psum_scatter(
        jnp.dot(active_all, down_proj, preferred_element_type=jnp.float32).astype(jnp.bfloat16),
        "req",
        scatter_dimension=0,
        tiled=True,
    )
    return (attended, ffn_out)


def solution(mesh):
    placed = (
        P("req", "head"),
        P("req", "head"),
        P("req", "head"),
        P("req", "head"),
        P("req", "head"),
        P(),
        P(),
        P(None, "req"),
        P("head", "req"),
        P(),
        P(None, ("req", "head")),
        P(None, ("req", "head")),
        P("req", "head"),
    )
    return jax.shard_map(
        body,
        mesh=mesh,
        in_specs=placed,
        out_specs=(P("head", "req"), P("req", "head")),
        check_vma=False,
    )
```

```python
import math

import jax
import jax.numpy as jnp
from jax import lax
from jax.experimental import pallas as pl
from jax.experimental.pallas import tpu as pltpu
from jax.sharding import PartitionSpec as P

D = 5120
HD = 128


def rope_tables(positions):
    half_dim = HD // 2
    freq_steps = jnp.arange(half_dim, dtype=jnp.float32)
    inverse = jnp.exp(freq_steps * (-2.0 * math.log(10000.0) / HD))
    angles = positions.astype(jnp.float32)[:, None] * inverse[None, :]
    return (jnp.cos(angles), jnp.sin(angles))


def dot_turned(left, right):
    return lax.dot_general(
        left, right, (((1,), (1,)), ((), ())), preferred_element_type=jnp.float32
    )


def swap_halves(v):
    half = HD // 2
    return jnp.concatenate([v[:, half:], v[:, :half]], axis=1)


def attend_pair(q_pair, k_pair, v_pair, key_rows, value_rows, cosine, sine, starts, ends):
    scale = HD ** (-0.5)
    owned = q_pair.shape[0]
    rows = key_rows.shape[0]
    rotated = []
    own = []
    for j in range(2):
        cols = slice(j * HD, (j + 1) * HD)
        q = q_pair[:, cols].astype(jnp.float32)
        k = k_pair[:, cols].astype(jnp.float32)
        q = (q * cosine + swap_halves(q) * sine).astype(jnp.bfloat16)
        k = (k * cosine + swap_halves(k) * sine).astype(jnp.bfloat16)
        rotated.append(q)
        own.append(
            jnp.sum(q.astype(jnp.float32) * k.astype(jnp.float32), axis=-1, keepdims=True) * scale
        )
    blank = jnp.zeros((owned, HD), jnp.bfloat16)
    both = jnp.concatenate(
        [
            jnp.concatenate([rotated[0], blank], axis=1),
            jnp.concatenate([blank, rotated[1]], axis=1),
        ],
        axis=0,
    )
    own = jnp.concatenate(own, axis=0)
    scores = dot_turned(both, key_rows) * scale
    starts = jnp.concatenate([starts] * 2, axis=0)
    ends = jnp.concatenate([ends] * 2, axis=0)
    places = lax.broadcasted_iota(jnp.int32, (2 * owned, rows), 1)
    member = (places >= starts) & (places < ends)
    masked = jnp.where(member, scores, -jnp.inf)
    top = jnp.maximum(jnp.max(masked, axis=-1, keepdims=True), own)
    weights = jnp.exp(masked - top)
    own_weight = jnp.exp(own - top)
    total = jnp.sum(weights, axis=-1, keepdims=True) + own_weight
    summed = jnp.dot(weights.astype(jnp.bfloat16), value_rows, preferred_element_type=jnp.float32)
    own_weight = own_weight.astype(jnp.bfloat16).astype(jnp.float32)
    heads = []
    for j in range(2):
        cols = slice(j * HD, (j + 1) * HD)
        part = slice(j * owned, (j + 1) * owned)
        value = v_pair[:, cols].astype(jnp.float32)
        heads.append((summed[part, cols] + own_weight[part] * value) / total[part])
    return jnp.concatenate(heads, axis=1).astype(jnp.bfloat16)


def attend_kernel(q_ref, k_ref, v_ref, kp_ref, vp_ref, cos_ref, sin_ref, st_ref, en_ref, out_ref):
    out_ref[...] = attend_pair(
        q_ref[...],
        k_ref[...],
        v_ref[...],
        kp_ref[...],
        vp_ref[...],
        cos_ref[...],
        sin_ref[...],
        st_ref[...],
        en_ref[...],
    )


def pick(table_row, chosen):
    places = lax.broadcasted_iota(jnp.int32, (chosen.shape[0], table_row.shape[1]), 1)
    hit = places.astype(jnp.float32) == chosen
    return jnp.sum(jnp.where(hit, table_row, 0.0), axis=1, keepdims=True)


def counting(first, count):
    return (first + lax.broadcasted_iota(jnp.int32, (count, 1), 0)).astype(jnp.float32)


def running_starts(column):
    count = column.shape[0]
    down = lax.broadcasted_iota(jnp.int32, (count, count), 0)
    across = lax.broadcasted_iota(jnp.int32, (count, count), 1)
    row = jnp.sum(jnp.where(down == across, column, 0.0), axis=0, keepdims=True)
    return jnp.sum(jnp.where(across < down, row, 0.0), axis=1, keepdims=True)


def attend_local(query_new, key_new, value_new, key_pool, value_pool, seg_lengths):
    owned, width = query_new.shape
    rows = key_pool.shape[0]
    cosine, sine = rope_tables(seg_lengths)
    cosine = jnp.concatenate([cosine, cosine], axis=1)
    sine = jnp.concatenate([-sine, sine], axis=1)
    ends = jnp.cumsum(seg_lengths)
    starts = ends - seg_lengths
    wide = 2 * HD
    slots = pl.BlockSpec((owned, wide), lambda i: (0, i))
    pool = pl.BlockSpec((rows, wide), lambda i: (0, i))
    table = pl.BlockSpec((owned, HD), lambda i: (0, 0))
    edge = pl.BlockSpec((owned, 1), lambda i: (0, 0))
    return pl.pallas_call(
        attend_kernel,
        grid=(width // wide,),
        in_specs=[slots, slots, slots, pool, pool, table, table, edge, edge],
        out_specs=slots,
        out_shape=jax.ShapeDtypeStruct((owned, width), jnp.bfloat16),
        compiler_params=pltpu.CompilerParams(vmem_limit_bytes=48 * 1024 * 1024),
        cost_estimate=pl.CostEstimate(
            flops=4 * owned * rows * width,
            bytes_accessed=4 * rows * width,
            transcendentals=owned * rows * width // HD,
        ),
    )(
        query_new,
        key_new,
        value_new,
        key_pool,
        value_pool,
        cosine,
        sine,
        starts[:, None],
        ends[:, None],
    )


def layer_kernel(
    length_ref,
    slot_ref,
    gain_ref,
    q_hbm,
    k_hbm,
    v_hbm,
    kp_hbm,
    vp_hbm,
    res_hbm,
    out_hbm,
    gate_hbm,
    up_hbm,
    down_hbm,
    attended_ref,
    ffn_ref,
    wo,
    wg,
    wu,
    wd,
    q_in,
    k_in,
    v_in,
    kp_in,
    vp_in,
    res_in,
    att_all,
    part,
    core_out,
    core_in,
    y_out,
    y_in,
    hidden,
    squares,
    acc_gate,
    acc_up,
    active,
    down_part,
    x_out,
    x_in,
    z_out,
    z_in,
    cos_tab,
    sin_tab,
    edge_tab,
    res_rows,
    gains,
    n_sem,
    kp_sem,
    vp_sem,
    w_sem,
    a_zs,
    a_zr,
    a_xs,
    a_xr,
    c_s,
    c_r,
    p_s,
    p_r,
    h_zs,
    h_zr,
    h_xs,
    h_xr,
    h_ys,
    h_yr,
    h_as,
    h_ar,
    h_bs,
    h_br,
    h_cs,
    h_cr,
    g_ys,
    g_yr,
    g_cs,
    g_cr,
    f_xs,
    f_xr,
    f_zs,
    f_zr,
):
    r = lax.axis_index("req")
    h = lax.axis_index("head")
    z = r // 2
    x = r % 2
    y = h // 2
    c = h % 2
    xn = 1 - x
    yn = 1 - y
    cn = 1 - c
    zs = [(z + k) % 4 for k in range(4)]
    to_x = (z * 2 + xn, h)
    to_y = (r, yn * 2 + c)
    to_c = (r, y * 2 + cn)
    to_z = [(zs[k] * 2 + x, h) for k in range(4)]
    f32 = jnp.float32
    bf16 = jnp.bfloat16
    sent = []

    def copy(src, dst, send_sem, recv_sem, device):
        return pltpu.make_async_remote_copy(
            src_ref=src,
            dst_ref=dst,
            send_sem=send_sem,
            recv_sem=recv_sem,
            device_id=device,
            device_id_type=pl.DeviceIdType.MESH,
        )

    def send(*args):
        one = copy(*args)
        one.start()
        sent.append(one)

    def arrived(dst, send_sem, recv_sem, device):
        copy(dst, dst, send_sem, recv_sem, device).wait_recv()

    wide = att_all.shape[3]
    pieces = att_all.shape[0]

    def pair_cols(j):
        return pl.ds(pl.multiple_of(j * wide, wide), wide)

    def pool_loads(j):
        slot = j % 2
        return (
            pltpu.make_async_copy(kp_hbm.at[:, pair_cols(j)], kp_in.at[slot], kp_sem.at[slot]),
            pltpu.make_async_copy(vp_hbm.at[:, pair_cols(j)], vp_in.at[slot], vp_sem.at[slot]),
        )

    new_loads = [
        pltpu.make_async_copy(src, dst, n_sem.at[i])
        for i, (src, dst) in enumerate(((q_hbm, q_in), (k_hbm, k_in), (v_hbm, v_in)))
    ]
    loads = [
        pltpu.make_async_copy(src, dst, w_sem.at[i])
        for i, (src, dst) in enumerate(
            ((out_hbm, wo), (gate_hbm, wg), (up_hbm, wu), (down_hbm, wd), (res_hbm, res_in))
        )
    ]
    barrier = pltpu.get_barrier_semaphore()
    for device in (to_z[1], to_z[2], to_z[3], to_x, to_y, to_c):
        pl.semaphore_signal(
            barrier, inc=1, device_id=device, device_id_type=pl.DeviceIdType.MESH
        )
    for load in new_loads:
        load.start()
    for j in range(2):
        for load in pool_loads(j):
            load.start()
    for load in (loads[0], loads[4], loads[1], loads[2], loads[3]):
        load.start()

    length_row = length_ref[...].astype(f32)
    owned = q_in.shape[0]
    slot_row = slot_ref[...].astype(f32)
    slot_len = pick(length_row, pick(slot_row, counting(r * owned, owned)))
    begin = running_starts(slot_len)
    starts = begin.astype(jnp.int32)
    ends = (begin + slot_len).astype(jnp.int32)
    lane = lax.broadcasted_iota(jnp.int32, (1, HD), 1)
    freq = (lane % (HD // 2)).astype(f32)
    angles = slot_len * jnp.exp(freq * (-2.0 * math.log(10000.0) / HD))
    cosine = jnp.cos(angles)
    sine = jnp.where(lane < HD // 2, -1.0, 1.0) * jnp.sin(angles)
    cos_tab[...] = cosine
    sin_tab[...] = sine
    edge_tab[0] = jnp.broadcast_to(starts, (owned, HD))
    edge_tab[1] = jnp.broadcast_to(ends, (owned, HD))
    part[...] = jnp.zeros_like(part)
    gains[...] = gain_ref[...].astype(f32)
    for load in new_loads:
        load.wait()
    pl.semaphore_wait(barrier, 6)

    def attention_step(j, carry):
        @pl.when(j < pieces)
        def _():
            for load in pool_loads(j):
                load.wait()
            slot = j % 2
            att_all[j, r] = attend_pair(
                q_in[:, pair_cols(j)],
                k_in[:, pair_cols(j)],
                v_in[:, pair_cols(j)],
                kp_in[slot],
                vp_in[slot],
                cos_tab[...],
                sin_tab[...],
                edge_tab[0][:, :1],
                edge_tab[1][:, :1],
            )

            @pl.when(j + 2 < pieces)
            def _():
                for load in pool_loads(j + 2):
                    load.start()

            mine = att_all.at[j, r]
            for k in (1, 3, 2):
                copy(mine, mine, a_zs.at[j * 4 + k], a_zr.at[j * 4 + z], to_z[k]).start()
            copy(mine, mine, a_xs.at[j * 4 + z], a_xr.at[j * 4 + z], to_x).start()

        @pl.when(j == pieces)
        def _():
            loads[4].wait()
            for i in range(2):
                chosen = pick(slot_row, counting((h * 2 + i) * owned, owned))
                places = lax.broadcasted_iota(jnp.int32, (owned, res_in.shape[0]), 1).astype(f32)
                hit = jnp.where(places == chosen, 1.0, 0.0).astype(bf16)
                picked = jnp.dot(hit, res_in[...], preferred_element_type=f32)
                res_rows[i * owned : (i + 1) * owned, :] = picked

        @pl.when((j >= 1) & (j < pieces + 1))
        def _():
            p = j - 1
            for k in (1, 3, 2):
                q = zs[k]
                mine = att_all.at[p, q * 2 + x]
                arrived(mine, a_zs.at[p * 4 + k], a_zr.at[p * 4 + q], to_z[k])
                copy(mine, mine, a_xs.at[p * 4 + q], a_xr.at[p * 4 + q], to_x).start()

        @pl.when(j == 2)
        def _():
            loads[0].wait()

        @pl.when(j >= 2)
        def _():
            p = j - 2
            for k in (0, 1, 3, 2):
                q = zs[k]
                arrived(
                    att_all.at[p, q * 2 + xn], a_xs.at[p * 4 + q], a_xr.at[p * 4 + q], to_x
                )
            every = att_all[p].reshape(4 * part.shape[1], wide)
            depth = pl.ds(pl.multiple_of(p * wide, wide), wide)
            part[...] += jnp.dot(every, wo[depth, :], preferred_element_type=f32).reshape(
                part.shape
            )

        return carry

    lax.fori_loop(0, pieces + 2, attention_step, 0)

    for qy in (yn, y):
        core_out[qy] = part[qy * 2 + cn].astype(bf16)
        send(core_out.at[qy], core_in.at[qy], c_s.at[qy], c_r.at[qy], to_c)
    arrived(core_in.at[yn], c_s.at[yn], c_r.at[yn], to_c)
    y_out[...] = (part[yn * 2 + c] + core_in[yn].astype(f32)).astype(bf16)
    send(y_out, y_in, p_s, p_r, to_y)
    arrived(core_in.at[y], c_s.at[y], c_r.at[y], to_c)
    total = part[h] + core_in[y].astype(f32) + res_rows[...]
    arrived(y_in, p_s, p_r, to_y)
    mine = (total + y_in[...].astype(f32)).astype(bf16)
    attended_ref[...] = mine
    quarter = mine.shape[0]
    half = quarter // 2
    hidden[r, pl.ds(h * quarter, quarter), :] = mine

    def chunk(q, cx, cy, cc):
        return hidden.at[q * 2 + cx, pl.ds((cy * 2 + cc) * quarter, quarter), :]

    def halved(q, cx, cy, cc, which):
        return hidden.at[
            q * 2 + cx, pl.ds((cy * 2 + cc) * quarter + which * half, half), :
        ]

    def to_core(block, q, i):
        send(block, block, h_cs.at[q * 5 + i], h_cr.at[q * 5 + i], to_c)

    def from_core(block, q, i):
        arrived(block, h_cs.at[q * 5 + i], h_cr.at[q * 5 + i], to_c)

    def spread(k):
        q = zs[k]
        block = chunk(q, x, y, c)
        if k:
            arrived(block, h_zs.at[k], h_zr.at[q], to_z[k])
        send(block, block, h_xs.at[q], h_xr.at[q], to_x)
        send(block, block, h_ys.at[q], h_yr.at[q], to_y)
        to_core(block, q, 0)

    def diagonal(k):
        q = zs[k]
        block = chunk(q, xn, y, c)
        arrived(block, h_xs.at[q], h_xr.at[q], to_x)
        piece = halved(q, xn, y, c, 1)
        send(piece, piece, h_bs.at[q], h_br.at[q], to_y)
        to_core(block, q, 1)
        block = chunk(q, x, yn, c)
        arrived(block, h_ys.at[q], h_yr.at[q], to_y)
        piece = halved(q, x, yn, c, 0)
        send(piece, piece, h_as.at[q], h_ar.at[q], to_x)
        to_core(block, q, 2)

    def finish(k):
        q = zs[k]
        piece = halved(q, xn, yn, c, 0)
        arrived(piece, h_as.at[q], h_ar.at[q], to_x)
        to_core(piece, q, 3)
        piece = halved(q, xn, yn, c, 1)
        arrived(piece, h_bs.at[q], h_br.at[q], to_y)
        to_core(piece, q, 4)

    def collect_near(k):
        q = zs[k]
        from_core(chunk(q, x, y, cn), q, 0)
        from_core(chunk(q, x, yn, cn), q, 2)

    def collect_far(k):
        q = zs[k]
        from_core(chunk(q, xn, y, cn), q, 1)
        from_core(halved(q, xn, yn, cn, 0), q, 3)
        from_core(halved(q, xn, yn, cn, 1), q, 4)

    width = mine.shape[1]
    tall = 2 * quarter

    def multiply(k, sides=(0, 1)):
        q = zs[k]

        def step(i, carry):
            rows = pl.ds(pl.multiple_of(i * tall, tall), tall)
            gate = up = square = None
            for cx in sides:
                at = q * 2 + cx
                broad = hidden[at, rows, :].astype(f32)
                gain = jnp.concatenate(
                    [gains[pl.ds(at * (width // 128) + j, 1), :] for j in range(width // 128)],
                    axis=1,
                )
                power = broad * broad
                for j in range(width // 128):
                    one = power[:, j * 128 : (j + 1) * 128]
                    square = one if square is None else square + one
                scaled = (broad * gain).astype(bf16)
                depth = pl.ds(pl.multiple_of(at * width, width), width)
                one = dot_turned(scaled, wg[:, depth])
                gate = one if gate is None else gate + one
                one = dot_turned(scaled, wu[:, depth])
                up = one if up is None else up + one
            if k == first:
                acc_gate[rows, :] = gate
                acc_up[rows, :] = up
                squares[rows, :] = square
            else:
                acc_gate[rows, :] += gate
                acc_up[rows, :] += up
                squares[rows, :] += square
            return carry

        lax.fori_loop(0, hidden.shape[1] // tall, step, 0)

    own_chunk = chunk(z, x, y, c)
    for k in (1, 3, 2):
        send(own_chunk, own_chunk, h_zs.at[k], h_zr.at[z], to_z[k])
    order = (0, 1, 3, 2)
    first = order[0]
    spread(order[0])
    loads[1].wait()
    loads[2].wait()
    for i in range(4):
        if i < 3:
            spread(order[i + 1])
        diagonal(order[i])
        if i:
            collect_near(order[i - 1])
            collect_far(order[i - 1])
            multiply(order[i - 1])
        finish(order[i])
    collect_near(order[3])
    multiply(order[3], (x,))
    collect_far(order[3])
    multiply(order[3], (xn,))

    def rows_of(q):
        return pl.ds(pl.multiple_of(q * quarter, quarter), quarter)

    late = (1, 3, 2, 0)
    hy = yn * 2 + c
    hc = y * 2 + cn
    hd = yn * 2 + cn
    for k in late:
        q = zs[k]
        mean = jnp.sum(squares[rows_of(q), :], axis=-1, keepdims=True) / D
        inverse = lax.rsqrt(mean + 1e-05)
        gate = acc_gate[rows_of(q), :] * inverse
        up = acc_up[rows_of(q), :] * inverse
        active[h, q] = (gate / (1.0 + jnp.exp(-gate)) * up).astype(bf16)
        block = active.at[h, q]
        send(block, block, g_ys.at[q], g_yr.at[q], to_y)
        send(block, block, g_cs.at[q], g_cr.at[q], to_c)
    loads[3].wait()
    units = active.shape[3]

    def reduce_x(k):
        q = zs[k]
        arrived(x_in.at[q], f_xs.at[q], f_xr.at[q], to_x)
        total = down_part[q, x] + x_in[q].astype(f32)
        if k:
            z_out[q] = total.astype(bf16)
            send(z_out.at[q], z_in.at[z], f_zs.at[q], f_zr.at[z], to_z[k])
            return None
        return total

    for i, k in enumerate(late):
        q = zs[k]
        block = active.at[hy, q]
        arrived(block, g_ys.at[q], g_yr.at[q], to_y)
        send(block, block, g_cs.at[4 + q], g_cr.at[4 + q], to_c)
        arrived(active.at[hc, q], g_cs.at[q], g_cr.at[q], to_c)
        arrived(active.at[hd, q], g_cs.at[4 + q], g_cr.at[4 + q], to_c)
        total = None
        for g in range(4):
            one = jnp.dot(
                active[g, q], wd[g * units : (g + 1) * units, :], preferred_element_type=f32
            )
            total = one if total is None else total + one
        down_part[q] = total.reshape(down_part.shape[1:])
        x_out[q] = down_part[q, xn].astype(bf16)
        send(x_out.at[q], x_in.at[q], f_xs.at[q], f_xr.at[q], to_x)
        if i:
            reduce_x(late[i - 1])
    total = reduce_x(0)
    for k in (1, 3, 2):
        arrived(z_in.at[zs[k]], f_zs.at[zs[k]], f_zr.at[zs[k]], to_z[k])
        total = total + z_in[zs[k]].astype(f32)
    ffn_ref[...] = total.astype(bf16)
    for one in sent:
        one.wait_send()

    def drain(j, carry):
        mine = att_all.at[j, r]
        for k in (1, 3, 2):
            copy(mine, mine, a_zs.at[j * 4 + k], a_zr.at[j * 4 + z], to_z[k]).wait_send()
        for k in range(4):
            q = zs[k]
            mine = att_all.at[j, q * 2 + x]
            copy(mine, mine, a_xs.at[j * 4 + q], a_xr.at[j * 4 + q], to_x).wait_send()
        return carry

    lax.fori_loop(0, pieces, drain, 0)


def layer_local(
    query_new,
    key_new,
    value_new,
    key_pool,
    value_pool,
    lengths,
    slot_request,
    residual,
    out_proj,
    norm_gain,
    gate_proj,
    up_proj,
    down_proj,
):
    owned, feats = query_new.shape
    rows = key_pool.shape[0]
    slots, width = residual.shape
    quarter = slots // 4
    wide = 2 * HD
    gate_proj = gate_proj.T
    up_proj = up_proj.T
    units, hid = gate_proj.shape
    deep, cols = down_proj.shape
    blocks = hid // width
    bf16 = jnp.bfloat16
    f32 = jnp.float32
    dma = pltpu.SemaphoreType.DMA
    vmem = pl.BlockSpec(memory_space=pltpu.VMEM)
    hbm = pl.BlockSpec(memory_space=pl.ANY)
    return pl.pallas_call(
        layer_kernel,
        out_shape=(
            jax.ShapeDtypeStruct((quarter, width), bf16),
            jax.ShapeDtypeStruct((owned, cols), bf16),
        ),
        in_specs=[vmem] * 3 + [hbm] * 10,
        out_specs=(vmem, vmem),
        scratch_shapes=[
            pltpu.VMEM(out_proj.shape, bf16),
            pltpu.VMEM(gate_proj.shape, bf16),
            pltpu.VMEM(up_proj.shape, bf16),
            pltpu.VMEM(down_proj.shape, bf16),
            pltpu.VMEM((owned, feats), bf16),
            pltpu.VMEM((owned, feats), bf16),
            pltpu.VMEM((owned, feats), bf16),
            pltpu.VMEM((2, rows, wide), bf16),
            pltpu.VMEM((2, rows, wide), bf16),
            pltpu.VMEM(residual.shape, bf16),
            pltpu.VMEM((feats // wide, 8, owned, wide), bf16),
            pltpu.VMEM((4, quarter, width), f32),
            pltpu.VMEM((2, quarter, width), bf16),
            pltpu.VMEM((2, quarter, width), bf16),
            pltpu.VMEM((quarter, width), bf16),
            pltpu.VMEM((quarter, width), bf16),
            pltpu.VMEM((blocks, 4 * quarter, width), bf16),
            pltpu.VMEM((4 * quarter, 128), f32),
            pltpu.VMEM((4 * quarter, units), f32),
            pltpu.VMEM((4 * quarter, units), f32),
            pltpu.VMEM((4, 4, quarter, units), bf16),
            pltpu.VMEM((4, 2, owned, cols), f32),
            pltpu.VMEM((4, owned, cols), bf16),
            pltpu.VMEM((4, owned, cols), bf16),
            pltpu.VMEM((4, owned, cols), bf16),
            pltpu.VMEM((4, owned, cols), bf16),
            pltpu.VMEM((owned, HD), f32),
            pltpu.VMEM((owned, HD), f32),
            pltpu.VMEM((2, owned, HD), jnp.int32),
            pltpu.VMEM((quarter, width), f32),
            pltpu.VMEM((hid // 128, 128), f32),
            dma((3,)),
            dma((2,)),
            dma((2,)),
            dma((5,)),
            dma((feats // wide * 4,)),
            dma((feats // wide * 4,)),
            dma((feats // wide * 4,)),
            dma((feats // wide * 4,)),
            dma((2,)),
            dma((2,)),
            dma,
            dma,
            dma((4,)),
            dma((4,)),
            dma((4,)),
            dma((4,)),
            dma((4,)),
            dma((4,)),
            dma((4,)),
            dma((4,)),
            dma((4,)),
            dma((4,)),
            dma((20,)),
            dma((20,)),
            dma((4,)),
            dma((4,)),
            dma((8,)),
            dma((8,)),
            dma((4,)),
            dma((4,)),
            dma((4,)),
            dma((4,)),
        ],
        compiler_params=pltpu.CompilerParams(
            collective_id=1, has_side_effects=True, vmem_limit_bytes=58 * 1024 * 1024
        ),
        cost_estimate=pl.CostEstimate(
            flops=2 * 4 * quarter * (2 * hid * units + deep * cols + feats * width),
            bytes_accessed=2 * (2 * hid * units + deep * cols + feats * width),
            transcendentals=4 * quarter * units,
        ),
    )(
        lengths.reshape(1, slots),
        slot_request.reshape(1, slots),
        norm_gain.reshape(hid // 128, 128),
        query_new,
        key_new,
        value_new,
        key_pool,
        value_pool,
        residual,
        out_proj,
        gate_proj,
        up_proj,
        down_proj,
    )

def body(
    query_new,
    key_new,
    value_new,
    key_pool,
    value_pool,
    lengths,
    slot_request,
    residual,
    out_proj,
    norm_gain,
    gate_proj,
    up_proj,
    down_proj,
):
    owned = query_new.shape[0]
    req_count = lax.axis_size("req")
    head_count = lax.axis_size("head")
    if (req_count, head_count) == (8, 4):
        return layer_local(
            query_new,
            key_new,
            value_new,
            key_pool,
            value_pool,
            lengths,
            slot_request,
            residual,
            out_proj,
            norm_gain,
            gate_proj,
            up_proj,
            down_proj,
        )
    first_slot = lax.axis_index("req") * owned
    my_requests = lax.dynamic_slice_in_dim(slot_request, first_slot, owned, 0)
    my_lengths = jnp.take(lengths, my_requests, axis=0)
    attention = attend_local(query_new, key_new, value_new, key_pool, value_pool, my_lengths)
    partial_sums = jnp.dot(
        lax.all_gather(attention, "req", axis=0, tiled=True),
        out_proj,
        preferred_element_type=jnp.float32,
    )
    summed = lax.psum_scatter(partial_sums, "head", scatter_dimension=0, tiled=True)
    quarter = summed.shape[0]
    quarter_slots = lax.dynamic_slice_in_dim(
        slot_request, lax.axis_index("head") * quarter, quarter, 0
    )
    attended = (jnp.take(residual, quarter_slots, axis=0).astype(jnp.float32) + summed).astype(
        jnp.bfloat16
    )
    column_width = attended.shape[1]
    gain_grid = norm_gain.astype(jnp.float32).reshape(req_count, 1, column_width)
    everywhere = lax.all_gather(attended[None], ("req", "head"), axis=0, tiled=True)
    hidden_grid = everywhere.reshape(req_count, head_count, quarter, column_width).astype(
        jnp.float32
    )
    squares = jnp.sum(hidden_grid * hidden_grid, axis=(0, 3))
    inverse = lax.rsqrt(squares / D + 1e-05)
    scaled = (hidden_grid * inverse[None, :, :, None] * gain_grid[:, None]).astype(jnp.bfloat16)
    col_block = gate_proj.shape[1]
    gate_pre = jnp.einsum(
        "rhbc,rcf->hbf",
        scaled,
        gate_proj.reshape(req_count, column_width, col_block),
        preferred_element_type=jnp.float32,
    )
    upward = jnp.einsum(
        "rhbc,rcf->hbf",
        scaled,
        up_proj.reshape(req_count, column_width, col_block),
        preferred_element_type=jnp.float32,
    )
    active = (jax.nn.silu(gate_pre) * upward).astype(jnp.bfloat16)
    gathered = lax.all_gather(active, "head", axis=2, tiled=True)
    active_all = gathered.reshape(head_count * quarter, head_count * col_block)
    ffn_out = lax.psum_scatter(
        jnp.dot(active_all, down_proj, preferred_element_type=jnp.float32).astype(jnp.bfloat16),
        "req",
        scatter_dimension=0,
        tiled=True,
    )
    return (attended, ffn_out)


def solution(mesh):
    placed = (
        P("req", "head"),
        P("req", "head"),
        P("req", "head"),
        P("req", "head"),
        P("req", "head"),
        P(),
        P(),
        P(None, "req"),
        P("head", "req"),
        P(),
        P(None, ("req", "head")),
        P(None, ("req", "head")),
        P("req", "head"),
    )
    return jax.shard_map(
        body,
        mesh=mesh,
        in_specs=placed,
        out_specs=(P("head", "req"), P("req", "head")),
        check_vma=False,
    )
```
